32 devices in a mesh: groups: 2 (over x), blk: 16 (over z, y, core).
Axes of the slice: x: 2, y: 2, z: 4, core: 2. Of those that a mesh axis runs over, the one named last changes fastest.
Arguments:
- embedding: bfloat16 [65536, 256], P(('groups', 'blk')), parts along dimension 0, may hold values from -0.7 to 0.7
- assignment: int32 [65536], P(('groups', 'blk')), parts along dimension 0, may hold values from 0 to 127, as said below
- kernel_rate: float32 [2], P('groups'), parts along dimension 0, may hold values from 0.6 to 1.6
Outputs:
- affinity: float32 [65536, 128], P(('groups', 'blk')), parts along dimension 0
- compact: float32 [256], P('groups'), parts along dimension 0
The draws below stay inside these ranges and needn't reach their ends.
There are 2 independent parts, one for each index of `groups`. The reference program is written for one: setup_inputs(seed, part) draws one part's arguments, and reference() takes and returns one part's arrays. A program takes and returns all parts, laid end to end along the dimension named above; each array names one. Nothing has to cross between parts.
Inputs may be any that keep to these rules, and one draw needn't show every extreme that they name: `assignment`: every cluster has at least one node.
All inputs are finite; a program needn't handle non-finite values.
Results may differ from the reference program's by a relative error of at most 0.0005.
Values may be sent and summed in bfloat16 or wider, within the bound.
A program may use at most 64 MiB of HBM per device.

```python
import math
import jax
import jax.numpy as jnp
from jax import lax

D = 256
CLUSTERS = 128
ROWS = 2048
NODES = 32768
N_BLK = 16


def draw_assignment(key, part):
    key = jax.random.fold_in(key, 3)
    label_key = jax.random.fold_in(key, 11)
    place_key = jax.random.fold_in(key, 12)
    labels = jax.random.randint(label_key, (NODES,), 0, CLUSTERS, dtype=jnp.int32)
    chosen = jax.random.permutation(place_key, NODES)[:CLUSTERS]
    return labels.at[chosen].set(jnp.arange(CLUSTERS, dtype=jnp.int32))


def draw_embedding(key, part):
    key = jax.random.fold_in(key, 5)
    places = 4 * (NODES // ROWS)
    parent_count = (places + 15) // 16
    parent_key = jax.random.fold_in(key, 21)
    child_key = jax.random.fold_in(key, 22)
    member_key = jax.random.fold_in(key, 23)
    spread_key = jax.random.fold_in(key, 24)
    noise_key = jax.random.fold_in(key, 25)
    parent_centres = jnp.clip(jax.random.normal(parent_key, (parent_count, D), jnp.float32), -4.0, 4.0) * (1.2 / 16.0)
    child_centres = jnp.clip(jax.random.normal(child_key, (places, D), jnp.float32), -4.0, 4.0) * (0.7 / 16.0)
    block_index = jnp.arange(NODES, dtype=jnp.int32) // ROWS
    community = (4 * block_index + jax.random.randint(member_key, (NODES,), 0, 24, dtype=jnp.int32)) % places
    centre = parent_centres[community // 16] + child_centres[community]
    spread = jnp.exp(jax.random.uniform(spread_key, (NODES, 1), jnp.float32, math.log(0.2), math.log(0.7)))
    noise = jnp.clip(jax.random.normal(noise_key, (NODES, D), jnp.float32), -4.0, 4.0)
    return (centre + spread * noise * (1.0 / 16.0)).astype(jnp.bfloat16)


def setup_inputs(seed: int = 0, part: int = 0) -> dict:
    streams_of = jax.random.split(jax.random.key(seed), 4)
    own_keys = jax.random.split(jax.random.fold_in(streams_of[3], part), 4)
    embedding = draw_embedding(jax.random.fold_in(jax.random.fold_in(streams_of[3], part), 71), part)
    assignment = draw_assignment(jax.random.fold_in(jax.random.fold_in(streams_of[3], part), 71), part)
    kernel_rate = jnp.clip(jnp.exp(jax.random.uniform(own_keys[2], (1,), jnp.float32, math.log(0.6), math.log(1.6))), 0.6, 1.6)
    return {"embedding": embedding, "assignment": assignment, "kernel_rate": kernel_rate}


def kernel_tile(left_rows, right_rows, decay):
    left_norm = jnp.sum(jnp.square(left_rows.astype(jnp.float32)), axis=1)
    right_norm = jnp.sum(jnp.square(right_rows.astype(jnp.float32)), axis=1)
    inner = lax.dot_general(left_rows, right_rows, (((1,), (1,)), ((), ())), preferred_element_type=jnp.float32)
    return jnp.exp(-decay * (left_norm[:, None] + right_norm[None, :] - 2.0 * inner)).astype(jnp.bfloat16)


def reference(embedding, assignment, kernel_rate):
    decay = kernel_rate[0]
    blocks = embedding.reshape(N_BLK, ROWS, D)
    labels_hot = (assignment[:, None] == jnp.arange(CLUSTERS, dtype=jnp.int32)[None, :]).astype(jnp.bfloat16)
    hot_blocks = labels_hot.reshape(N_BLK, ROWS, CLUSTERS)

    def per_block(index):
        rows = blocks[index]
        own_hot = hot_blocks[index]
        total = jnp.dot(kernel_tile(rows, rows, decay), own_hot, preferred_element_type=jnp.float32)
        owed = []
        for offset in (1, 2):
            partner = ((index + offset) % N_BLK).astype(jnp.int32)
            tile = kernel_tile(rows, blocks[partner], decay)
            total = total + jnp.dot(tile, hot_blocks[partner], preferred_element_type=jnp.float32)
            owed.append(lax.dot_general(tile, own_hot, (((0,), (0,)), ((), ())), preferred_element_type=jnp.float32))
        return total, owed[0], owed[1]

    total, near_owed, far_owed = lax.map(per_block, jnp.arange(N_BLK, dtype=jnp.int32))
    total = total + jnp.roll(near_owed, 1, axis=0) + jnp.roll(far_owed, 2, axis=0)
    total = total.reshape(NODES, CLUSTERS)
    affinity = total * (CLUSTERS / (5.0 * ROWS))
    hot_float = labels_hot.astype(jnp.float32)
    mass = jnp.sum(total * hot_float, axis=0)
    count = jnp.sum(hot_float, axis=0)
    compact = mass * (CLUSTERS / (5.0 * ROWS)) / count
    return affinity, compact
```

```python
import functools
import math
import jax
import jax.numpy as jnp
from jax import lax
from jax.experimental import pallas as pl
from jax.experimental.pallas import tpu as pltpu
from jax.sharding import PartitionSpec as P

CLUSTERS = 128
CHUNKS = 4
META = 256
NT = (((1,), (1,)), ((), ()))
NEXT_TO = (-2, -1, 1, 2)

OTHER, NEAR, FAR, LENT = range(4)
SCHEDULE = (
    ("own", 0), ("own", 1), ("own", 2), ("own", 3), ("near", 0),
    (OTHER, 0), (OTHER, 1), (OTHER, 2), ("near", 1),
    (OTHER, 3), (NEAR, 0), ("far", 0), (NEAR, 1), ("near", 2),
    (NEAR, 2), (FAR, 0), ("far", 1), (LENT, 0), ("near", 3),
    (NEAR, 3), (FAR, 1), ("far", 2), (LENT, 1), (FAR, 2), ("far", 3),
    (LENT, 2), (FAR, 3), (LENT, 3),
)


def kernel(n, factor, rate_ref, emb_ref, lab_ref, total_ref, compact_ref,
           held, meta, col, hot, parts,
           block_send, block_recv, other_send, other_recv, meta_send, meta_recv,
           part_send, part_recv):
    rows = emb_ref.shape[0]
    size = rows // CHUNKS
    me = lax.axis_index("blk")
    core = lax.rem(me, 2)
    chip = me // 2
    odd = lax.rem(chip, 2)
    step = 1 - 2 * odd
    other = me + 1 - 2 * core
    across = me + 2 * step
    onward = lax.rem(me + 4 * step + n, n)
    lend_near = lax.rem(chip + core, 2) == 0

    barrier = pltpu.get_barrier_semaphore()

    def greet(o, _):
        pl.semaphore_signal(barrier, inc=1, device_id={"blk": lax.rem(me + o, n)},
                            device_id_type=pl.DeviceIdType.MESH)
        return 0

    lax.fori_loop(1, n, greet, 0)

    rate = rate_ref[0] * math.log2(math.e)
    own_meta = 2
    meta[own_meta, 8:16, :] = lab_ref[...].astype(jnp.float32)
    ones = jnp.ones((8, emb_ref.shape[1]), jnp.bfloat16)
    for c in range(CHUNKS):
        e = emb_ref[c * size:(c + 1) * size, :].astype(jnp.float32)
        sq = e * e
        col[c * size:(c + 1) * size, :] = jnp.sum(sq, axis=1, keepdims=True) * -rate
        high = sq.astype(jnp.bfloat16)
        low = (sq - high.astype(jnp.float32)).astype(jnp.bfloat16)
        line = (lax.dot_general(ones, high, NT, preferred_element_type=jnp.float32)
                + lax.dot_general(ones, low, NT, preferred_element_type=jnp.float32)) * -rate
        for q in range(size // META):
            r = c * (size // META) + q
            meta[own_meta, r:r + 1, :] = line[0:1, q * META:(q + 1) * META]

    pl.semaphore_wait(barrier, n - 1)

    def remote(src, dst, send, recv, peer):
        return pltpu.make_async_remote_copy(
            src_ref=src, dst_ref=dst, send_sem=send, recv_sem=recv,
            device_id={"blk": peer}, device_id_type=pl.DeviceIdType.MESH)

    def piece(c):
        return pl.ds(c * size, size)

    to_near = [remote(emb_ref.at[piece(c)], held.at[NEAR, piece(c)],
                      block_send.at[0, c], block_recv.at[0, c], across) for c in range(CHUNKS)]
    to_far = [remote(held.at[NEAR, piece(c)], held.at[FAR, piece(c)],
                     block_send.at[1, c], block_recv.at[1, c], onward) for c in range(CHUNKS)]
    lend_slot = jnp.where(lend_near, NEAR, FAR)
    to_lent = [remote(held.at[lend_slot, piece(c)], held.at[LENT, piece(c)],
                      block_send.at[2, c], block_recv.at[2, c], other) for c in range(CHUNKS)]
    to_other = remote(emb_ref, held.at[OTHER], other_send, other_recv, other)
    to_meta = [remote(meta.at[own_meta], meta.at[2 - o], meta_send.at[i], meta_recv.at[i],
                      lax.rem(me + o + n, n)) for i, o in enumerate(NEXT_TO)]

    for copy in to_meta:
        copy.start()
    to_other.start()
    for copy in to_near:
        copy.start()

    def hot_line(slot, c):
        first = c * (size // META)
        lab = jnp.concatenate(
            [meta[slot, 8 + first + q:9 + first + q, :] for q in range(size // META)], axis=1)
        line = lax.broadcasted_iota(jnp.int32, (CLUSTERS, size), 0).astype(jnp.float32)
        return line == lab

    for c in range(CHUNKS):
        picked = jnp.where(hot_line(own_meta, c), 1.0, 0.0)
        hot[c * size:(c + 1) * size, :] = jnp.transpose(picked)

    total_ref[...] = jnp.zeros_like(total_ref)
    slots = {
        OTHER: 3 - 2 * core, NEAR: 2 + 2 * step, FAR: 2 - 2 * step, LENT: 1 + 2 * core,
    }

    def work(block, slot, c):
        first = c * (size // META)
        norm = jnp.concatenate(
            [meta[slot, first + q:first + q + 1, :] for q in range(size // META)], axis=1)
        right_hot = hot_line(slot, c).astype(jnp.float32).astype(jnp.bfloat16)
        right = block[piece(c), :]

        def left(i, _):
            r = pl.ds(pl.multiple_of(i * size, size), size)
            inner = lax.dot_general(emb_ref[r, :], right, NT, preferred_element_type=jnp.float32)
            tile = jnp.exp2(inner * (2.0 * rate) + (col[r, :] + norm)).astype(jnp.bfloat16)
            total_ref[r, :] += lax.dot_general(
                tile, right_hot, NT, preferred_element_type=jnp.float32)
            return 0

        lax.fori_loop(0, rows // size, left, 0, unroll=2)

    for what, c in SCHEDULE:
        if what == "own":
            work(emb_ref, own_meta, c)
        elif what == "near":
            to_near[c].wait_recv()
            to_far[c].start()

            @pl.when(lend_near)
            def _():
                to_lent[c].start()
        elif what == "far":
            to_far[c].wait_recv()

            @pl.when(jnp.logical_not(lend_near))
            def _():
                to_lent[c].start()
        else:
            if what == OTHER and c == 0:
                to_other.wait_recv()
                for copy in to_meta:
                    copy.wait_recv()
            if what == LENT:
                to_lent[c].wait_recv()
            work(held.at[what], slots[what], c)

    total = total_ref[...]
    own_hot = hot[...]
    mass = jnp.sum(total * own_hot, axis=0, keepdims=True)
    count = jnp.sum(own_hot, axis=0, keepdims=True)
    parts[me, 0:1, :] = mass
    parts[me, 1:2, :] = count

    def to_part(o):
        return remote(parts.at[me], parts.at[me], part_send.at[o], part_recv.at[o],
                      lax.rem(me + o, n))

    def send_part(o, _):
        to_part(o).start()
        return 0

    lax.fori_loop(1, n, send_part, 0)
    total_ref[...] = total * factor
    for copy in to_meta + [to_other] + to_near + to_far + to_lent:
        copy.wait_send()

    def end_part(o, _):
        source = lax.rem(me - o + n, n)
        remote(parts.at[me], parts.at[source], part_send.at[o], part_recv.at[o],
               lax.rem(me + o, n)).wait()
        return 0

    lax.fori_loop(1, n, end_part, 0)

    masses = jnp.sum(parts[:, 0:1, :], axis=0)
    counts = jnp.sum(parts[:, 1:2, :], axis=0)
    compact_ref[...] = masses * factor / counts


def local(n, embedding, assignment, kernel_rate):
    rows, width = embedding.shape
    factor = CLUSTERS / (5.0 * rows)
    dma = pltpu.SemaphoreType.DMA
    affinity, compact = pl.pallas_call(
        functools.partial(kernel, n, factor),
        out_shape=(jax.ShapeDtypeStruct((rows, CLUSTERS), jnp.float32),
                   jax.ShapeDtypeStruct((1, CLUSTERS), jnp.float32)),
        in_specs=[pl.BlockSpec(memory_space=pltpu.SMEM),
                  pl.BlockSpec(memory_space=pltpu.VMEM),
                  pl.BlockSpec(memory_space=pltpu.VMEM)],
        out_specs=[pl.BlockSpec(memory_space=pltpu.VMEM)] * 2,
        scratch_shapes=[
            pltpu.VMEM((4, rows, width), jnp.bfloat16),
            pltpu.VMEM((5, 16, META), jnp.float32),
            pltpu.VMEM((rows, 1), jnp.float32),
            pltpu.VMEM((rows, CLUSTERS), jnp.float32),
            pltpu.VMEM((n, 8, CLUSTERS), jnp.float32),
            dma((3, CHUNKS)), dma((3, CHUNKS)), dma, dma, dma((4,)), dma((4,)),
            dma((n,)), dma((n,)),
        ],
        compiler_params=pltpu.CompilerParams(
            collective_id=0, has_side_effects=True, vmem_limit_bytes=48 * 2**20),
        name="affinities",
    )(kernel_rate, embedding, assignment.reshape(rows // META, META))
    return affinity, compact.reshape(CLUSTERS)


def solution(mesh):
    n = mesh.shape["blk"]
    in_specs = (P(("groups", "blk"), None), P(("groups", "blk")), P("groups"))
    out_specs = (P(("groups", "blk"), None), P("groups"))
    return jax.shard_map(functools.partial(local, n), mesh=mesh, in_specs=in_specs,
                         out_specs=out_specs, check_vma=False)
```

```python
import functools
import math
import jax
import jax.numpy as jnp
from jax import lax
from jax.experimental import pallas as pl
from jax.experimental.pallas import tpu as pltpu
from jax.sharding import PartitionSpec as P

CLUSTERS = 128
META = 256
NT = (((1,), (1,)), ((), ()))
NEXT_TO = (-2, -1, 1, 2)

OTHER, NEAR, FAR, LENT, OWN = range(5)
QUARTERS = 4
ORDER = (
    (OWN, 0), (OWN, 1), (OWN, 2), (OWN, 3), (OTHER, 0), (OTHER, 1), (OTHER, 2),
    (NEAR, 0), (FAR, 0), (LENT, 0), (NEAR, 1), (FAR, 1), (LENT, 1), (NEAR, 2),
    (OTHER, 3), (FAR, 2), (LENT, 2), (NEAR, 3), (FAR, 3), (LENT, 3),
)


def lookup(step, values):
    found = jnp.int32(values[0])
    for k, value in enumerate(values):
        if k and value != values[k - 1]:
            found = jnp.where(step >= k, jnp.int32(value), found)
    return found


def kernel(n, factor, rate_ref, emb_ref, lab_ref, total_ref, compact_ref,
           held, meta, line, sums, parts, own_copy,
           block_send, block_recv, other_send, other_recv, meta_send, meta_recv,
           part_send, part_recv):
    rows = emb_ref.shape[0]
    size = rows // QUARTERS
    chunks = rows // META
    me = lax.axis_index("blk")
    core = lax.rem(me, 2)
    chip = me // 2
    odd = lax.rem(chip, 2)
    step_to = 1 - 2 * odd
    other = me + 1 - 2 * core
    across = me + 2 * step_to
    onward = lax.rem(me + 4 * step_to + n, n)
    lend_near = lax.rem(chip + core, 2) == 0

    barrier = pltpu.get_barrier_semaphore()

    def greet(o, _):
        pl.semaphore_signal(barrier, inc=1, device_id={"blk": lax.rem(me + o, n)},
                            device_id_type=pl.DeviceIdType.MESH)
        return 0

    lax.fori_loop(1, n, greet, 0)
    own = pltpu.make_async_copy(emb_ref, held.at[OWN], own_copy)
    own.start()
    meta[2] = lab_ref[...]
    sums[...] = jnp.zeros_like(sums)
    pl.semaphore_wait(barrier, n - 1)

    def remote(src, dst, send, recv, peer):
        return pltpu.make_async_remote_copy(
            src_ref=src, dst_ref=dst, send_sem=send, recv_sem=recv,
            device_id={"blk": peer}, device_id_type=pl.DeviceIdType.MESH)

    def piece(c):
        return pl.ds(pl.multiple_of(c * META, META), META)

    def to_near(c):
        return remote(emb_ref.at[piece(c)], held.at[NEAR, piece(c)],
                      block_send.at[0, c], block_recv.at[0, c], across)

    def to_far(c):
        return remote(held.at[NEAR, piece(c)], held.at[FAR, piece(c)],
                      block_send.at[1, c], block_recv.at[1, c], onward)

    lend_slot = jnp.where(lend_near, NEAR, FAR)

    def to_lent(c):
        return remote(held.at[lend_slot, piece(c)], held.at[LENT, piece(c)],
                      block_send.at[2, c], block_recv.at[2, c], other)

    to_other = remote(emb_ref, held.at[OTHER], other_send, other_recv, other)
    to_meta = [remote(lab_ref, meta.at[2 - o], meta_send.at[i], meta_recv.at[i],
                      lax.rem(me + o + n, n)) for i, o in enumerate(NEXT_TO)]

    to_near(0).start()
    to_other.start()
    for copy in to_meta:
        copy.start()

    def send_near(c, _):
        to_near(c).start()
        return 0

    lax.fori_loop(1, chunks, send_near, 0)
    own.wait()

    rate = rate_ref[0] * math.log2(math.e)
    ones = jnp.ones((8, emb_ref.shape[1]), jnp.bfloat16)

    def own_norm(c, _):
        r = pl.ds(pl.multiple_of(c * size, size), size)
        e = held[OWN, r, :].astype(jnp.float32)
        sq = e * e
        high = sq.astype(jnp.bfloat16)
        low = (sq - high.astype(jnp.float32)).astype(jnp.bfloat16)
        norm = (lax.dot_general(ones, high, NT, preferred_element_type=jnp.float32)
                + lax.dot_general(ones, low, NT, preferred_element_type=jnp.float32))
        line[:, r] = norm[0:1, :] * -rate
        return 0

    lax.fori_loop(0, QUARTERS, own_norm, 0)

    def hot_rows(slot, c):
        first = c * (size // META)
        lab = jnp.concatenate(
            [meta[slot, pl.ds(first + q, 1), :] for q in range(size // META)], axis=1)
        return lax.broadcasted_iota(jnp.int32, (CLUSTERS, size), 0) == lab

    def as_line(x):
        width = x.shape[1]
        folded = x[:, 0:CLUSTERS]
        for q in range(1, width // CLUSTERS):
            folded = folded + x[:, q * CLUSTERS:(q + 1) * CLUSTERS]
        return jnp.sum(jnp.transpose(folded), axis=0, keepdims=True)

    count = sum(as_line(jnp.where(hot_rows(2, c), 1.0, 0.0)) for c in range(QUARTERS))
    parts[me, 1:2, :] = count

    blocks = [block for block, _ in ORDER]
    quarters = [c for _, c in ORDER]

    def work(step, _):
        @pl.when(jnp.logical_and(lax.rem(step, 2) == 0,
                                 jnp.logical_and(step >= 2, step <= 16)))
        def _():
            c = (step - 2) // 2
            to_near(c).wait_recv()
            to_far(c).start()

            @pl.when(lend_near)
            def _():
                to_lent(c).start()

        @pl.when(jnp.logical_or(
            jnp.logical_and(lax.rem(step, 2) == 1,
                            jnp.logical_and(step >= 5, step <= 17)), step == 18))
        def _():
            c = (step - 4) // 2
            to_far(c).wait_recv()

            @pl.when(jnp.logical_not(lend_near))
            def _():
                to_lent(c).start()

        @pl.when(step == 4)
        def _():
            to_other.wait_recv()
            for copy in to_meta:
                copy.wait_recv()

        block = lookup(step, blocks)
        quarter = lookup(step, quarters)

        @pl.when(block == LENT)
        def _():
            to_lent(2 * quarter).wait_recv()
            to_lent(2 * quarter + 1).wait_recv()

        slot = jnp.where(block == OWN, 2, jnp.where(
            block == OTHER, 3 - 2 * core, jnp.where(
                block == NEAR, 2 + 2 * step_to, jnp.where(
                    block == FAR, 2 - 2 * step_to, 1 + 2 * core))))
        right = held[block, pl.ds(pl.multiple_of(quarter * size, size), size), :]
        right_hot = hot_rows(slot, quarter).astype(jnp.float32).astype(jnp.bfloat16)
        wide = right.astype(jnp.float32)
        norm = jnp.sum(wide * wide, axis=1, keepdims=True) * -rate
        inner = lax.dot_general(right, held[OWN], NT, preferred_element_type=jnp.float32)
        tile = jnp.exp2(inner * (2.0 * rate) + (norm + line[...])).astype(jnp.bfloat16)
        sums[...] += jnp.dot(right_hot, tile, preferred_element_type=jnp.float32)
        return 0

    lax.fori_loop(0, len(ORDER), work, 0)

    mass = sum(as_line(jnp.where(hot_rows(2, c), sums[:, c * size:(c + 1) * size], 0.0))
               for c in range(QUARTERS))
    parts[me, 0:1, :] = mass

    def send_part(o, _):
        remote(parts.at[me], parts.at[me], part_send.at[o], part_recv.at[o],
               lax.rem(me + o, n)).start()
        return 0

    lax.fori_loop(1, n, send_part, 0)
    for q in range(rows // CLUSTERS):
        r = slice(q * CLUSTERS, (q + 1) * CLUSTERS)
        total_ref[r, :] = jnp.transpose(sums[:, r]) * factor
    for copy in to_meta + [to_other]:
        copy.wait_send()

    def end_sends(c, _):
        to_near(c).wait_send()
        to_far(c).wait_send()
        to_lent(c).wait_send()
        return 0

    lax.fori_loop(0, chunks, end_sends, 0)

    def end_part(o, _):
        source = lax.rem(me - o + n, n)
        remote(parts.at[me], parts.at[source], part_send.at[o], part_recv.at[o],
               lax.rem(me + o, n)).wait()
        return 0

    lax.fori_loop(1, n, end_part, 0)

    masses = jnp.sum(parts[:, 0:1, :], axis=0)
    counts = jnp.sum(parts[:, 1:2, :], axis=0)
    compact_ref[...] = masses * factor / counts


def local(n, embedding, assignment, kernel_rate):
    rows, width = embedding.shape
    factor = CLUSTERS / (5.0 * rows)
    dma = pltpu.SemaphoreType.DMA
    affinity, compact = pl.pallas_call(
        functools.partial(kernel, n, factor),
        out_shape=(jax.ShapeDtypeStruct((rows, CLUSTERS), jnp.float32),
                   jax.ShapeDtypeStruct((1, CLUSTERS), jnp.float32)),
        in_specs=[pl.BlockSpec(memory_space=pltpu.SMEM),
                  pl.BlockSpec(memory_space=pl.ANY),
                  pl.BlockSpec(memory_space=pltpu.VMEM)],
        out_specs=[pl.BlockSpec(memory_space=pltpu.VMEM)] * 2,
        scratch_shapes=[
            pltpu.VMEM((5, rows, width), jnp.bfloat16),
            pltpu.VMEM((5, rows // META, META), jnp.int32),
            pltpu.VMEM((1, rows), jnp.float32),
            pltpu.VMEM((CLUSTERS, rows), jnp.float32),
            pltpu.VMEM((n, 8, CLUSTERS), jnp.float32),
            dma, dma((3, rows // META)), dma((3, rows // META)), dma, dma, dma((4,)), dma((4,)),
            dma((n,)), dma((n,)),
        ],
        compiler_params=pltpu.CompilerParams(
            collective_id=0, has_side_effects=True, vmem_limit_bytes=48 * 2**20),
        name="affinities",
    )(kernel_rate, embedding, assignment.reshape(rows // META, META))
    return affinity, compact.reshape(CLUSTERS)


def solution(mesh):
    n = mesh.shape["blk"]
    in_specs = (P(("groups", "blk"), None), P(("groups", "blk")), P("groups"))
    out_specs = (P(("groups", "blk"), None), P("groups"))
    return jax.shard_map(functools.partial(local, n), mesh=mesh, in_specs=in_specs,
                         out_specs=out_specs, check_vma=False)
```

```python
import functools
import math
import jax
import jax.numpy as jnp
from jax import lax
from jax.experimental import pallas as pl
from jax.experimental.pallas import tpu as pltpu
from jax.sharding import PartitionSpec as P

CLUSTERS = 128
META = 256
NT = (((1,), (1,)), ((), ()))
NEXT_TO = (-2, -1, 1, 2)

OTHER, NEAR, FAR, LENT, OWN = range(5)
QUARTERS = 4
ORDER = (
    (OWN, 0), (OWN, 1), (OWN, 2), (OWN, 3), (OTHER, 0), (OTHER, 1), (OTHER, 2),
    (NEAR, 0), (FAR, 0), (LENT, 0), (NEAR, 1), (FAR, 1), (LENT, 1), (NEAR, 2),
    (OTHER, 3), (FAR, 2), (LENT, 2), (NEAR, 3), (FAR, 3), (LENT, 3),
)


def lookup(step, values):
    found = jnp.int32(values[0])
    for k, value in enumerate(values):
        if k and value != values[k - 1]:
            found = jnp.where(step >= k, jnp.int32(value), found)
    return found


def kernel(n, factor, rate_ref, emb_ref, lab_ref, total_ref, compact_ref,
           held, meta, line, sums, parts, own_copy,
           block_send, block_recv, other_send, other_recv, meta_send, meta_recv,
           part_send, part_recv):
    rows = emb_ref.shape[0]
    size = rows // QUARTERS
    chunks = rows // META
    me = lax.axis_index("blk")
    core = lax.rem(me, 2)
    chip = me // 2
    odd = lax.rem(chip, 2)
    step_to = 1 - 2 * odd
    other = me + 1 - 2 * core
    across = me + 2 * step_to
    onward = lax.rem(me + 4 * step_to + n, n)
    lend_near = lax.rem(chip + core, 2) == 0

    barrier = pltpu.get_barrier_semaphore()

    def greet(o, _):
        pl.semaphore_signal(barrier, inc=1, device_id={"blk": lax.rem(me + o, n)},
                            device_id_type=pl.DeviceIdType.MESH)
        return 0

    lax.fori_loop(1, n, greet, 0)
    own = pltpu.make_async_copy(emb_ref, held.at[OWN], own_copy)
    own.start()
    meta[2] = lab_ref[...]
    sums[...] = jnp.zeros_like(sums)
    pl.semaphore_wait(barrier, n - 1)

    def remote(src, dst, send, recv, peer):
        return pltpu.make_async_remote_copy(
            src_ref=src, dst_ref=dst, send_sem=send, recv_sem=recv,
            device_id={"blk": peer}, device_id_type=pl.DeviceIdType.MESH)

    def piece(c):
        return pl.ds(pl.multiple_of(c * META, META), META)

    def to_near(c):
        return remote(emb_ref.at[piece(c)], held.at[NEAR, piece(c)],
                      block_send.at[0, c], block_recv.at[0, c], across)

    def to_far(c):
        return remote(held.at[NEAR, piece(c)], held.at[FAR, piece(c)],
                      block_send.at[1, c], block_recv.at[1, c], onward)

    lend_slot = jnp.where(lend_near, NEAR, FAR)

    def to_lent(c):
        return remote(held.at[lend_slot, piece(c)], held.at[LENT, piece(c)],
                      block_send.at[2, c], block_recv.at[2, c], other)

    to_other = remote(emb_ref, held.at[OTHER], other_send, other_recv, other)
    to_meta = [remote(lab_ref, meta.at[2 - o], meta_send.at[i], meta_recv.at[i],
                      lax.rem(me + o + n, n)) for i, o in enumerate(NEXT_TO)]

    to_near(0).start()
    to_other.start()
    for copy in to_meta:
        copy.start()

    def send_near(c, _):
        to_near(c).start()
        return 0

    lax.fori_loop(1, chunks, send_near, 0)
    own.wait()

    rate = rate_ref[0] * math.log2(math.e)
    ones = jnp.ones((8, emb_ref.shape[1]), jnp.bfloat16)

    def own_norm(c, _):
        r = pl.ds(pl.multiple_of(c * size, size), size)
        e = held[OWN, r, :].astype(jnp.float32)
        sq = e * e
        high = sq.astype(jnp.bfloat16)
        low = (sq - high.astype(jnp.float32)).astype(jnp.bfloat16)
        norm = (lax.dot_general(ones, high, NT, preferred_element_type=jnp.float32)
                + lax.dot_general(ones, low, NT, preferred_element_type=jnp.float32))
        line[:, r] = norm[0:1, :] * -rate
        return 0

    lax.fori_loop(0, QUARTERS, own_norm, 0)

    def hot_rows(slot, c):
        first = c * (size // META)
        lab = jnp.concatenate(
            [meta[slot, pl.ds(first + q, 1), :] for q in range(size // META)], axis=1)
        return lax.broadcasted_iota(jnp.int32, (CLUSTERS, size), 0) == lab

    def as_line(x):
        width = x.shape[1]
        folded = x[:, 0:CLUSTERS]
        for q in range(1, width // CLUSTERS):
            folded = folded + x[:, q * CLUSTERS:(q + 1) * CLUSTERS]
        return jnp.sum(jnp.transpose(folded), axis=0, keepdims=True)

    count = sum(as_line(jnp.where(hot_rows(2, c), 1.0, 0.0)) for c in range(QUARTERS))
    parts[me, 1:2, :] = count

    blocks = [block for block, _ in ORDER]
    quarters = [c for _, c in ORDER]

    def work(step, _):
        @pl.when(jnp.logical_and(lax.rem(step, 2) == 0,
                                 jnp.logical_and(step >= 2, step <= 16)))
        def _():
            c = (step - 2) // 2
            to_near(c).wait_recv()
            to_far(c).start()

            @pl.when(lend_near)
            def _():
                to_lent(c).start()

        @pl.when(jnp.logical_or(
            jnp.logical_and(lax.rem(step, 2) == 1,
                            jnp.logical_and(step >= 5, step <= 17)), step == 18))
        def _():
            c = (step - 4) // 2
            to_far(c).wait_recv()

            @pl.when(jnp.logical_not(lend_near))
            def _():
                to_lent(c).start()

        @pl.when(step == 4)
        def _():
            to_other.wait_recv()
            for copy in to_meta:
                copy.wait_recv()

        block = lookup(step, blocks)
        quarter = lookup(step, quarters)

        @pl.when(block == LENT)
        def _():
            to_lent(2 * quarter).wait_recv()
            to_lent(2 * quarter + 1).wait_recv()

        slot = jnp.where(block == OWN, 2, jnp.where(
            block == OTHER, 3 - 2 * core, jnp.where(
                block == NEAR, 2 + 2 * step_to, jnp.where(
                    block == FAR, 2 - 2 * step_to, 1 + 2 * core))))
        right = held[block, pl.ds(pl.multiple_of(quarter * size, size), size), :]
        right_hot = hot_rows(slot, quarter).astype(jnp.float32).astype(jnp.bfloat16)
        wide = right.astype(jnp.float32)
        norm = jnp.sum(wide * wide, axis=1, keepdims=True) * -rate
        inner = lax.dot_general(right, held[OWN], NT, preferred_element_type=jnp.float32)
        tile = jnp.exp2(inner * (2.0 * rate) + (norm + line[...])).astype(jnp.bfloat16)
        sums[...] += jnp.dot(right_hot, tile, preferred_element_type=jnp.float32)
        return 0

    lax.fori_loop(0, len(ORDER), work, 0)

    mass = sum(as_line(jnp.where(hot_rows(2, c), sums[:, c * size:(c + 1) * size], 0.0))
               for c in range(QUARTERS))
    parts[me, 0:1, :] = mass

    def send_part(o, _):
        remote(parts.at[me], parts.at[me], part_send, part_recv, lax.rem(me + o, n)).start()
        return 0

    lax.fori_loop(1, n, send_part, 0)
    for q in range(rows // CLUSTERS):
        r = slice(q * CLUSTERS, (q + 1) * CLUSTERS)
        total_ref[r, :] = jnp.transpose(sums[:, r]) * factor
    for copy in to_meta + [to_other]:
        copy.wait_send()

    def end_sends(c, _):
        to_near(c).wait_send()
        to_far(c).wait_send()
        to_lent(c).wait_send()
        return 0

    lax.fori_loop(0, chunks, end_sends, 0)

    all_parts = remote(parts.at[pl.ds(0, n - 1)], parts.at[pl.ds(0, n - 1)],
                       part_send, part_recv, other)
    all_parts.wait_send()
    all_parts.wait_recv()

    masses = jnp.sum(parts[:, 0:1, :], axis=0)
    counts = jnp.sum(parts[:, 1:2, :], axis=0)
    compact_ref[...] = masses * factor / counts


def local(n, embedding, assignment, kernel_rate):
    rows, width = embedding.shape
    factor = CLUSTERS / (5.0 * rows)
    dma = pltpu.SemaphoreType.DMA
    affinity, compact = pl.pallas_call(
        functools.partial(kernel, n, factor),
        out_shape=(jax.ShapeDtypeStruct((rows, CLUSTERS), jnp.float32),
                   jax.ShapeDtypeStruct((1, CLUSTERS), jnp.float32)),
        in_specs=[pl.BlockSpec(memory_space=pltpu.SMEM),
                  pl.BlockSpec(memory_space=pl.ANY),
                  pl.BlockSpec(memory_space=pltpu.VMEM)],
        out_specs=[pl.BlockSpec(memory_space=pltpu.VMEM)] * 2,
        scratch_shapes=[
            pltpu.VMEM((5, rows, width), jnp.bfloat16),
            pltpu.VMEM((5, rows // META, META), jnp.int32),
            pltpu.VMEM((1, rows), jnp.float32),
            pltpu.VMEM((CLUSTERS, rows), jnp.float32),
            pltpu.VMEM((n, 8, CLUSTERS), jnp.float32),
            dma, dma((3, rows // META)), dma((3, rows // META)), dma, dma, dma((4,)), dma((4,)),
            dma, dma,
        ],
        compiler_params=pltpu.CompilerParams(
            collective_id=0, has_side_effects=True, vmem_limit_bytes=48 * 2**20),
        name="affinities",
    )(kernel_rate, embedding, assignment.reshape(rows // META, META))
    return affinity, compact.reshape(CLUSTERS)


def solution(mesh):
    n = mesh.shape["blk"]
    in_specs = (P(("groups", "blk"), None), P(("groups", "blk")), P("groups"))
    out_specs = (P(("groups", "blk"), None), P("groups"))
    return jax.shard_map(functools.partial(local, n), mesh=mesh, in_specs=in_specs,
                         out_specs=out_specs, check_vma=False)
```

```python
import functools
import math
import jax
import jax.numpy as jnp
from jax import lax
from jax.experimental import pallas as pl
from jax.experimental.pallas import tpu as pltpu
from jax.sharding import PartitionSpec as P

CLUSTERS = 128
META = 256
NT = (((1,), (1,)), ((), ()))
NEXT_TO = (-2, -1, 1, 2)

OTHER, NEAR, FAR, LENT, OWN = range(5)
QUARTERS = 4
ORDER = (
    (OWN, 0), (OWN, 1), (OWN, 2), (OWN, 3), (OTHER, 0), (OTHER, 1), (OTHER, 2),
    (NEAR, 0), (FAR, 0), (LENT, 0), (NEAR, 1), (FAR, 1), (LENT, 1), (NEAR, 2),
    (OTHER, 3), (FAR, 2), (LENT, 2), (NEAR, 3), (FAR, 3), (LENT, 3),
)


def lookup(step, values):
    found = jnp.int32(values[0])
    for k, value in enumerate(values):
        if k and value != values[k - 1]:
            found = jnp.where(step >= k, jnp.int32(value), found)
    return found


def kernel(n, factor, rate_ref, emb_ref, lab_ref, total_ref, compact_ref,
           held, meta, line, sums, parts, own_copy,
           block_send, block_recv, other_send, other_recv, meta_send, meta_recv,
           part_send, part_recv):
    rows = emb_ref.shape[0]
    size = rows // QUARTERS
    chunks = rows // META
    me = lax.axis_index("blk")
    core = lax.rem(me, 2)
    chip = me // 2
    odd = lax.rem(chip, 2)
    step_to = 1 - 2 * odd
    other = me + 1 - 2 * core
    across = me + 2 * step_to
    onward = lax.rem(me + 4 * step_to + n, n)
    lend_near = lax.rem(chip + core, 2) == 0

    barrier = pltpu.get_barrier_semaphore()

    def greet(o, _):
        pl.semaphore_signal(barrier, inc=1, device_id={"blk": lax.rem(me + o, n)},
                            device_id_type=pl.DeviceIdType.MESH)
        return 0

    lax.fori_loop(1, n, greet, 0)
    own = pltpu.make_async_copy(emb_ref, held.at[OWN], own_copy)
    own.start()
    meta[2] = lab_ref[...]
    sums[...] = jnp.zeros_like(sums)
    pl.semaphore_wait(barrier, n - 1)

    def remote(src, dst, send, recv, peer):
        return pltpu.make_async_remote_copy(
            src_ref=src, dst_ref=dst, send_sem=send, recv_sem=recv,
            device_id={"blk": peer}, device_id_type=pl.DeviceIdType.MESH)

    def piece(c):
        return pl.ds(pl.multiple_of(c * META, META), META)

    def to_near(c):
        return remote(emb_ref.at[piece(c)], held.at[NEAR, piece(c)],
                      block_send.at[0, c], block_recv.at[0, c], across)

    def to_far(c):
        return remote(held.at[NEAR, piece(c)], held.at[FAR, piece(c)],
                      block_send.at[1, c], block_recv.at[1, c], onward)

    lend_slot = jnp.where(lend_near, NEAR, FAR)

    def to_lent(c):
        return remote(held.at[lend_slot, piece(c)], held.at[LENT, piece(c)],
                      block_send.at[2, c], block_recv.at[2, c], other)

    to_other = remote(emb_ref, held.at[OTHER], other_send, other_recv, other)
    to_meta = [remote(lab_ref, meta.at[2 - o], meta_send.at[i], meta_recv.at[i],
                      lax.rem(me + o + n, n)) for i, o in enumerate(NEXT_TO)]

    to_other.start()
    to_near(0).start()
    for copy in to_meta:
        copy.start()

    def send_near(c, _):
        to_near(c).start()
        return 0

    lax.fori_loop(1, chunks, send_near, 0)
    own.wait()

    rate = rate_ref[0] * math.log2(math.e)
    ones = jnp.ones((8, emb_ref.shape[1]), jnp.bfloat16)

    def own_norm(c, _):
        r = pl.ds(pl.multiple_of(c * size, size), size)
        e = held[OWN, r, :].astype(jnp.float32)
        sq = e * e
        high = sq.astype(jnp.bfloat16)
        low = (sq - high.astype(jnp.float32)).astype(jnp.bfloat16)
        norm = (lax.dot_general(ones, high, NT, preferred_element_type=jnp.float32)
                + lax.dot_general(ones, low, NT, preferred_element_type=jnp.float32))
        line[:, r] = norm[0:1, :] * -rate
        return 0

    lax.fori_loop(0, QUARTERS, own_norm, 0)

    def hot_rows(slot, c):
        first = c * (size // META)
        lab = jnp.concatenate(
            [meta[slot, pl.ds(first + q, 1), :] for q in range(size // META)], axis=1)
        return lax.broadcasted_iota(jnp.int32, (CLUSTERS, size), 0) == lab

    def as_line(x):
        width = x.shape[1]
        folded = x[:, 0:CLUSTERS]
        for q in range(1, width // CLUSTERS):
            folded = folded + x[:, q * CLUSTERS:(q + 1) * CLUSTERS]
        return jnp.sum(jnp.transpose(folded), axis=0, keepdims=True)

    count = sum(as_line(jnp.where(hot_rows(2, c), 1.0, 0.0)) for c in range(QUARTERS))
    parts[me, 1:2, :] = count

    blocks = [block for block, _ in ORDER]
    quarters = [c for _, c in ORDER]

    def work(step, _):
        @pl.when(jnp.logical_and(lax.rem(step, 2) == 0,
                                 jnp.logical_and(step >= 2, step <= 16)))
        def _():
            c = (step - 2) // 2
            to_near(c).wait_recv()
            to_far(c).start()

            @pl.when(lend_near)
            def _():
                to_lent(c).start()

        @pl.when(jnp.logical_or(
            jnp.logical_and(lax.rem(step, 2) == 1,
                            jnp.logical_and(step >= 5, step <= 17)), step == 18))
        def _():
            c = (step - 4) // 2
            to_far(c).wait_recv()

            @pl.when(jnp.logical_not(lend_near))
            def _():
                to_lent(c).start()

        @pl.when(step == 4)
        def _():
            to_other.wait_recv()
            for copy in to_meta:
                copy.wait_recv()

        block = lookup(step, blocks)
        quarter = lookup(step, quarters)

        @pl.when(block == LENT)
        def _():
            to_lent(2 * quarter).wait_recv()
            to_lent(2 * quarter + 1).wait_recv()

        slot = jnp.where(block == OWN, 2, jnp.where(
            block == OTHER, 3 - 2 * core, jnp.where(
                block == NEAR, 2 + 2 * step_to, jnp.where(
                    block == FAR, 2 - 2 * step_to, 1 + 2 * core))))
        right = held[block, pl.ds(pl.multiple_of(quarter * size, size), size), :]
        right_hot = hot_rows(slot, quarter).astype(jnp.float32).astype(jnp.bfloat16)
        wide = right.astype(jnp.float32)
        norm = jnp.sum(wide * wide, axis=1, keepdims=True) * -rate
        inner = lax.dot_general(right, held[OWN], NT, preferred_element_type=jnp.float32)
        tile = jnp.exp2(inner * (2.0 * rate) + (norm + line[...])).astype(jnp.bfloat16)
        sums[...] += jnp.dot(right_hot, tile, preferred_element_type=jnp.float32)
        return 0

    lax.fori_loop(0, len(ORDER), work, 0)

    mass = sum(as_line(jnp.where(hot_rows(2, c), sums[:, c * size:(c + 1) * size], 0.0))
               for c in range(QUARTERS))
    parts[me, 0:1, :] = mass

    def send_part(o, _):
        remote(parts.at[me], parts.at[me], part_send, part_recv, lax.rem(me + o, n)).start()
        return 0

    lax.fori_loop(1, n, send_part, 0)
    for q in range(rows // CLUSTERS):
        r = slice(q * CLUSTERS, (q + 1) * CLUSTERS)
        total_ref[r, :] = jnp.transpose(sums[:, r]) * factor
    for copy in to_meta + [to_other]:
        copy.wait_send()

    def end_sends(c, _):
        to_near(c).wait_send()
        to_far(c).wait_send()
        to_lent(c).wait_send()
        return 0

    lax.fori_loop(0, chunks, end_sends, 0)

    all_parts = remote(parts.at[pl.ds(0, n - 1)], parts.at[pl.ds(0, n - 1)],
                       part_send, part_recv, other)
    all_parts.wait_send()
    all_parts.wait_recv()

    masses = jnp.sum(parts[:, 0:1, :], axis=0)
    counts = jnp.sum(parts[:, 1:2, :], axis=0)
    compact_ref[...] = masses * factor / counts


def local(n, embedding, assignment, kernel_rate):
    rows, width = embedding.shape
    factor = CLUSTERS / (5.0 * rows)
    dma = pltpu.SemaphoreType.DMA
    affinity, compact = pl.pallas_call(
        functools.partial(kernel, n, factor),
        out_shape=(jax.ShapeDtypeStruct((rows, CLUSTERS), jnp.float32),
                   jax.ShapeDtypeStruct((1, CLUSTERS), jnp.float32)),
        in_specs=[pl.BlockSpec(memory_space=pltpu.SMEM),
                  pl.BlockSpec(memory_space=pltpu.HBM),
                  pl.BlockSpec(memory_space=pltpu.VMEM)],
        out_specs=[pl.BlockSpec(memory_space=pltpu.VMEM)] * 2,
        scratch_shapes=[
            pltpu.VMEM((5, rows, width), jnp.bfloat16),
            pltpu.VMEM((5, rows // META, META), jnp.int32),
            pltpu.VMEM((1, rows), jnp.float32),
            pltpu.VMEM((CLUSTERS, rows), jnp.float32),
            pltpu.VMEM((n, 8, CLUSTERS), jnp.float32),
            dma, dma((3, rows // META)), dma((3, rows // META)), dma, dma, dma((4,)), dma((4,)),
            dma, dma,
        ],
        compiler_params=pltpu.CompilerParams(
            collective_id=0, has_side_effects=True, vmem_limit_bytes=48 * 2**20),
        name="affinities",
    )(kernel_rate, embedding, assignment.reshape(rows // META, META))
    return affinity, compact.reshape(CLUSTERS)


def solution(mesh):
    n = mesh.shape["blk"]
    in_specs = (P(("groups", "blk"), None), P(("groups", "blk")), P("groups"))
    out_specs = (P(("groups", "blk"), None), P("groups"))
    return jax.shard_map(functools.partial(local, n), mesh=mesh, in_specs=in_specs,
                         out_specs=out_specs, check_vma=False)
```
